32 devices in a mesh: seq: 8 (over z, y), dp: 4 (over x, core).
Axes of the slice: x: 2, y: 2, z: 4, core: 2. Of those that a mesh axis runs over, the one named last changes fastest.
Arguments:
- query_input: bfloat16 [4, 4096, 2048], P('dp', 'seq'), may hold values from -6 to 6
- key_input: bfloat16 [4, 4096, 2048], P('dp', 'seq'), may hold values from -6 to 6
- value_input: bfloat16 [4, 4096, 2048], P('dp', 'seq'), may hold values from -6 to 6
- grad_output: bfloat16 [4, 4096, 2048], P('dp', 'seq'), may hold values from -6 to 6
- out_weight: bfloat16 [2048, 2048], P(('seq', 'dp')), may hold values from -0.125 to 0.125
- norm_gain: float32 [2048], replicated, may hold values from 0.1 to 1.9
Outputs:
- result: bfloat16 [4, 4096, 2048], P('dp', 'seq')
- grad_query: bfloat16 [4, 4096, 2048], P('dp', 'seq')
- grad_key: bfloat16 [4, 4096, 2048], P('dp', 'seq')
- grad_value: bfloat16 [4, 4096, 2048], P('dp', 'seq')
- grad_weight: float32 [2048, 2048], P(('seq', 'dp'))
The draws below stay inside these ranges and needn't reach their ends.
All inputs are finite; a program needn't handle non-finite values.
Results may differ from the reference program's by a relative error of at most 0.015.
Values may be sent and summed in bfloat16 or wider, within the bound.
A program may use at most 192 MiB of HBM per device.

```python
import jax
import jax.numpy as jnp
from jax import lax

HEADS = 16
HEAD_DIM = 128
OUT_COLS = 2048
BLOCK = 512
FEATURES = 2048
LENGTH = 4096
BATCH = 4


def level_of(stream_key, dims, cuts, low, top_value):
    def one(axis_at, blocks):
        draws = jax.random.uniform(jax.random.fold_in(jax.random.fold_in(stream_key, 6), axis_at), (blocks,), jnp.float32, low / len(cuts), top_value / len(cuts))
        return jnp.repeat(jnp.exp(draws), dims[axis_at] // blocks).reshape((-1,) + (1,) * (len(dims) - axis_at - 1))

    level = one(*cuts[0])
    for cut in cuts[1:]:
        level = level * one(*cut)
    return level


def bell_draw(key, shape, spread, reach, shards=(), dtype=jnp.bfloat16):
    values = spread * jax.random.normal(key, shape, jnp.float32)
    if shards:
        values = values * level_of(key, shape, shards, -0.22, 0.18)
    return jnp.clip(values, -reach, reach).astype(dtype)


def setup_inputs(seed: int = 0) -> dict:
    key_of = jax.random.split(jax.random.key(seed), 7)
    return {
        "query_input": bell_draw(key_of[0], (BATCH, LENGTH, FEATURES), 1.0, 6.0, ((0, 4), (1, 8))),
        "key_input": bell_draw(key_of[1], (BATCH, LENGTH, FEATURES), 1.0, 6.0, ((0, 4), (1, 8))),
        "value_input": bell_draw(key_of[2], (BATCH, LENGTH, FEATURES), 1.0, 6.0, ((0, 4), (1, 8))),
        "grad_output": bell_draw(key_of[3], (BATCH, LENGTH, OUT_COLS), 1.0, 6.0, ((0, 4), (1, 8))),
        "out_weight": bell_draw(key_of[4], (FEATURES, OUT_COLS), FEATURES ** -0.5, 0.125, ((0, 32),)),
        "norm_gain": jnp.clip(1.0 + 0.18 * jax.random.normal(key_of[5], (FEATURES,), jnp.float32), 0.1, 1.9),
    }


epsilon = 1e-06

def silu_slope(inputs):
    sigmoid_value = jax.nn.sigmoid(inputs)
    return sigmoid_value * (1.0 + inputs * (1.0 - sigmoid_value))

def causal_product(left, right):
    scores = jnp.einsum('ihd,jhd->hij', left.astype(jnp.float32), right.astype(jnp.float32))
    length_now = left.shape[0]
    causal = jnp.arange(length_now)[:, None] >= jnp.arange(length_now)[None, :]
    return jnp.where(causal[None], scores, 0.0)

def product(form, left, right):
    return jnp.einsum(form, left.astype(jnp.float32), right.astype(jnp.float32))

def one_sequence(pieces):
    query_input, key_input, value_input, grad_result, out_weight, norm_gain = pieces
    blocks = LENGTH // BLOCK
    query_raw = query_input.astype(jnp.float32)
    key_raw = key_input.astype(jnp.float32)
    feat_query = jax.nn.silu(query_raw).astype(jnp.bfloat16).reshape(blocks, BLOCK, HEADS, HEAD_DIM)
    feat_key = jax.nn.silu(key_raw).astype(jnp.bfloat16).reshape(blocks, BLOCK, HEADS, HEAD_DIM)
    value_blocks = value_input.reshape(blocks, BLOCK, HEADS, HEAD_DIM)
    zero_state = jnp.zeros((HEADS, HEAD_DIM, HEAD_DIM), jnp.float32)

    def forward_step(state, items):
        query_block, key_block, value_block = items
        state_low = state.astype(jnp.bfloat16)
        score_block = causal_product(query_block, key_block).astype(jnp.bfloat16)
        inside = product('hij,jhe->ihe', score_block, value_block)
        carried = product('ihd,hde->ihe', query_block, state_low)
        update = product('jhd,jhe->hde', key_block, value_block)
        return (state + update, (inside + carried, state_low))
    unused, (attention, prefix) = lax.scan(forward_step, zero_state, (feat_query, feat_key, value_blocks))
    attention = attention.reshape(LENGTH, FEATURES)
    radius = jnp.sqrt(lax.optimization_barrier(jnp.mean(attention * attention, axis=-1, keepdims=True)) + epsilon)
    normed = attention / radius
    mixed = (normed * norm_gain).astype(jnp.bfloat16)
    result = jnp.dot(mixed, out_weight, preferred_element_type=jnp.float32).astype(jnp.bfloat16)
    grad_mixed = jnp.dot(grad_result, out_weight.T, preferred_element_type=jnp.float32)
    grad_hat = grad_mixed * norm_gain
    grad_att = (grad_hat - normed * lax.optimization_barrier(jnp.mean(grad_hat * normed, axis=-1, keepdims=True))) / radius
    grad_att = grad_att.astype(jnp.bfloat16).reshape(blocks, BLOCK, HEADS, HEAD_DIM)

    def backward_step(later, items):
        query_block, key_block, value_block, grad_block, state_low = items
        later_low = later.astype(jnp.bfloat16)
        score_block = causal_product(query_block, key_block).astype(jnp.bfloat16)
        grad_scores = causal_product(grad_block, value_block).astype(jnp.bfloat16)
        grad_fq = product('hij,jhd->ihd', grad_scores, key_block) + product('ihe,hde->ihd', grad_block, state_low)
        grad_fk = product('hij,ihd->jhd', grad_scores, query_block) + product('jhe,hde->jhd', value_block, later_low)
        grad_fv = product('hij,ihe->jhe', score_block, grad_block) + product('jhd,hde->jhe', key_block, later_low)
        update = product('ihd,ihe->hde', query_block, grad_block)
        return (later + update, (grad_fq, grad_fk, grad_fv))
    unused, (grad_fq, grad_fk, grad_fv) = lax.scan(backward_step, zero_state, (feat_query, feat_key, value_blocks, grad_att, prefix), reverse=True)
    grad_query = (grad_fq.reshape(LENGTH, FEATURES) * silu_slope(query_raw)).astype(jnp.bfloat16)
    grad_key = (grad_fk.reshape(LENGTH, FEATURES) * silu_slope(key_raw)).astype(jnp.bfloat16)
    grad_value = grad_fv.reshape(LENGTH, FEATURES).astype(jnp.bfloat16)
    weight_term = jnp.dot(mixed.T, grad_result, preferred_element_type=jnp.float32)
    return (result, grad_query, grad_key, grad_value, weight_term)

def reference(query_input, key_input, value_input, grad_output, out_weight, norm_gain):

    def run(items):
        return one_sequence(items + (out_weight, norm_gain))
    result, grad_query, grad_key, grad_value, terms = lax.map(run, (query_input, key_input, value_input, grad_output))
    grad_weight = lax.optimization_barrier(jnp.sum(terms, axis=0))
    return (result, grad_query, grad_key, grad_value, grad_weight)
```

```python
import functools

import jax
import jax.numpy as jnp
from jax import lax
from jax.experimental import pallas as pl
from jax.experimental.pallas import tpu as pltpu
from jax.sharding import PartitionSpec as P

HEAD_DIM = 128
epsilon = 1e-06
MESH = pl.DeviceIdType.MESH
BF16 = jnp.bfloat16
F32 = jnp.float32
VMEM_LIMIT = 48 * 1024 * 1024


def dot(left, right, contract):
    return lax.dot_general(
        left, right, ((contract[:1], contract[1:]), ((), ())), preferred_element_type=F32
    )


def params(**more):
    return pltpu.CompilerParams(vmem_limit_bytes=VMEM_LIMIT, **more)


def head_cols(head):
    return slice(head * HEAD_DIM, (head + 1) * HEAD_DIM)


def causal(rows):
    return lax.broadcasted_iota(jnp.int32, (rows, rows), 0) >= lax.broadcasted_iota(
        jnp.int32, (rows, rows), 1
    )


def state_kernel(group, k_ref, v_ref, fk_ref, state_ref):
    raw = k_ref[...].astype(F32)
    fk = (raw * jax.nn.sigmoid(raw)).astype(BF16)
    fk_ref[...] = fk
    for head in range(group):
        cols = head_cols(head)
        state_ref[cols, :] = dot(fk[:, cols], v_ref[:, cols], (0, 0)).astype(BF16)


def local_state(key, value):
    tokens, features = key.shape
    group = 4
    width = group * HEAD_DIM
    spec = pl.BlockSpec((tokens, width), lambda i: (0, i))
    return pl.pallas_call(
        functools.partial(state_kernel, group),
        grid=(features // width,),
        in_specs=[spec, spec],
        out_specs=[spec, pl.BlockSpec((width, HEAD_DIM), lambda i: (i, 0))],
        out_shape=[
            jax.ShapeDtypeStruct((tokens, features), BF16),
            jax.ShapeDtypeStruct((features, HEAD_DIM), BF16),
        ],
        compiler_params=params(),
        name="local_state",
    )(key, value)


def carry_kernel(count, backward, x_ref, out_ref, got, sums, res, s1, r1, s2, r2):
    me = lax.axis_index("seq")
    part = x_ref.shape[0] // count

    def rows_of(index):
        return pl.ds(pl.multiple_of(index * part, part), part)

    barrier = pltpu.get_barrier_semaphore()
    for step in range(1, count):
        pl.semaphore_signal(
            barrier, inc=1, device_id={"seq": lax.rem(me + step, count)}, device_id_type=MESH
        )
    pl.semaphore_wait(barrier, count - 1)

    def send(step, source, target, send_sem, recv_sem):
        return pltpu.make_async_remote_copy(
            src_ref=source,
            dst_ref=target,
            send_sem=send_sem.at[step],
            recv_sem=recv_sem.at[step],
            device_id={"seq": lax.rem(me + step, count)},
            device_id_type=MESH,
        )

    first = []
    for step in range(1, count):
        peer = lax.rem(me + step, count)
        copy = send(step, x_ref.at[rows_of(peer)], got.at[me], s1, r1)
        copy.start()
        first.append(copy)
    got[me] = x_ref[rows_of(me), :]
    for copy in first:
        copy.wait_recv()
    total = jnp.zeros((part, x_ref.shape[1]), F32)
    order = range(count)
    for position in reversed(order) if backward else order:
        sums[position] = total.astype(BF16)
        total = total + got[position].astype(F32)
    second = []
    for step in range(1, count):
        peer = lax.rem(me + step, count)
        copy = send(step, sums.at[peer], res.at[rows_of(me)], s2, r2)
        copy.start()
        second.append(copy)
    res[rows_of(me), :] = sums[me]
    for copy in first:
        copy.wait_send()
    for copy in second:
        copy.wait_recv()
    out_ref[...] = res[...]
    for copy in second:
        copy.wait_send()


def carried(state, backward):
    count = lax.axis_size("seq")
    rows, cols = state.shape
    vmem = pl.BlockSpec(memory_space=pltpu.VMEM)
    sems = [pltpu.SemaphoreType.DMA((count,))] * 4
    return pl.pallas_call(
        functools.partial(carry_kernel, count, backward),
        in_specs=[vmem],
        out_specs=vmem,
        out_shape=jax.ShapeDtypeStruct((rows, cols), BF16),
        scratch_shapes=[
            pltpu.VMEM((count, rows // count, cols), BF16),
            pltpu.VMEM((count, rows // count, cols), BF16),
            pltpu.VMEM((rows, cols), BF16),
        ]
        + sems,
        compiler_params=params(collective_id=int(backward), has_side_effects=True),
        name="carry_later" if backward else "carry_earlier",
    )(state)


def forward_kernel(
    group, q_ref, fk_ref, v_ref, state_ref, gain_ref, fq_ref, mixed_ref, normed_ref, radius_ref,
    att, squares,
):
    step = pl.program_id(0)
    rows = q_ref.shape[0]
    raw = q_ref[...].astype(F32)
    fq = (raw * jax.nn.sigmoid(raw)).astype(BF16)
    fq_ref[...] = fq
    keep = causal(rows)

    @pl.when(step == 0)
    def _():
        squares[...] = jnp.zeros_like(squares)

    width = group * HEAD_DIM
    for head in range(group):
        cols = head_cols(head)
        scores = dot(fq[:, cols], fk_ref[:, cols], (1, 1))
        scores = jnp.where(keep, scores, 0.0).astype(BF16)
        out = dot(scores, v_ref[:, cols], (1, 0)) + dot(fq[:, cols], state_ref[cols, :], (1, 0))
        start = pl.multiple_of(step * width + head * HEAD_DIM, HEAD_DIM)
        att[:, pl.ds(start, HEAD_DIM)] = out
        squares[...] += out * out

    @pl.when(step == pl.num_programs(0) - 1)
    def _():
        features = att.shape[1]
        mean = jnp.sum(squares[...], axis=-1, keepdims=True) / features
        radius = jnp.sqrt(mean + epsilon)
        radius_ref[...] = jnp.broadcast_to(radius, radius_ref.shape)
        inverse = 1.0 / radius
        for start in range(0, features, 256):
            cols = slice(start, start + 256)
            normed = att[:, cols] * inverse
            normed_ref[:, cols] = normed.astype(BF16)
            mixed_ref[:, cols] = (normed * gain_ref[:, cols]).astype(BF16)


def forward(query, fk, value, state, gain):
    tokens, features = query.shape
    group = 2
    width = group * HEAD_DIM
    spec = pl.BlockSpec((tokens, width), lambda i: (0, i))
    whole = pl.BlockSpec((tokens, features), lambda i: (0, 0))
    wide = jax.ShapeDtypeStruct((tokens, features), BF16)
    return pl.pallas_call(
        functools.partial(forward_kernel, group),
        grid=(features // width,),
        in_specs=[
            spec,
            spec,
            spec,
            pl.BlockSpec((width, HEAD_DIM), lambda i: (i, 0)),
            pl.BlockSpec((1, features), lambda i: (0, 0)),
        ],
        out_specs=[spec, whole, whole, pl.BlockSpec((tokens, HEAD_DIM), lambda i: (0, 0))],
        out_shape=[wide, wide, wide, jax.ShapeDtypeStruct((tokens, HEAD_DIM), F32)],
        scratch_shapes=[pltpu.VMEM((tokens, features), F32), pltpu.VMEM((tokens, HEAD_DIM), F32)],
        compiler_params=params(),
        name="forward",
    )(query, fk, value, state, gain)


def project_kernel(
    go_ref, mixed_ref, normed_ref, radius_ref, fq_ref, weight_ref, gain_ref,
    result_ref, ga_ref, state_ref, total,
):
    step = pl.program_id(0)
    features = mixed_ref.shape[1]
    grad_mixed = dot(go_ref[...], weight_ref[...], (1, 1))
    grad_hat = grad_mixed * gain_ref[...]
    normed = normed_ref[...].astype(F32)
    inner = jnp.mean(grad_hat * normed, axis=-1, keepdims=True)
    inverse = 1.0 / radius_ref[:, :1]
    grad_att = ((grad_hat - normed * inner) * inverse).astype(BF16)
    ga_ref[...] = grad_att

    @pl.when(step == 0)
    def _():
        total[...] = jnp.zeros_like(total)

    for head in range(features // HEAD_DIM):
        cols = head_cols(head)
        total[cols, :] += dot(fq_ref[:, cols], grad_att[:, cols], (0, 0))
    result_ref[...] = dot(mixed_ref[...], weight_ref[...], (1, 0)).astype(BF16)

    @pl.when(step == pl.num_programs(0) - 1)
    def _():
        state_ref[...] = total[...].astype(BF16)


def project(grad_output, mixed, normed, radius, fq, weight, gain):
    tokens, features = mixed.shape
    out_cols = weight.shape[1]
    rows = 256
    narrow = pl.BlockSpec((rows, features), lambda i: (i, 0))
    outs = pl.BlockSpec((rows, out_cols), lambda i: (i, 0))
    whole = lambda i: (0, 0)
    return pl.pallas_call(
        project_kernel,
        grid=(tokens // rows,),
        in_specs=[
            outs,
            narrow,
            narrow,
            pl.BlockSpec((rows, HEAD_DIM), lambda i: (i, 0)),
            narrow,
            pl.BlockSpec(weight.shape, whole),
            pl.BlockSpec((1, features), whole),
        ],
        out_specs=[outs, narrow, pl.BlockSpec((features, HEAD_DIM), whole)],
        out_shape=[
            jax.ShapeDtypeStruct((tokens, out_cols), BF16),
            jax.ShapeDtypeStruct((tokens, features), BF16),
            jax.ShapeDtypeStruct((features, HEAD_DIM), BF16),
        ],
        scratch_shapes=[pltpu.VMEM((features, HEAD_DIM), F32)],
        compiler_params=params(),
        name="project",
    )(grad_output, mixed, normed, radius, fq, weight, gain)


def backward_kernel(
    group, q_ref, k_ref, v_ref, ga_ref, state_ref, later_ref, gq_ref, gk_ref, gv_ref
):
    rows = q_ref.shape[0]
    keep = causal(rows)
    for head in range(group):
        cols = head_cols(head)
        q_raw = q_ref[:, cols].astype(F32)
        k_raw = k_ref[:, cols].astype(F32)
        q_sig = jax.nn.sigmoid(q_raw)
        k_sig = jax.nn.sigmoid(k_raw)
        fq = (q_raw * q_sig).astype(BF16)
        fk = (k_raw * k_sig).astype(BF16)
        value = v_ref[:, cols]
        grad = ga_ref[:, cols]
        state = state_ref[cols, :]
        later = later_ref[cols, :]
        scores = jnp.where(keep, dot(fq, fk, (1, 1)), 0.0).astype(BF16)
        grad_scores = jnp.where(keep, dot(grad, value, (1, 1)), 0.0).astype(BF16)
        grad_fq = dot(grad_scores, fk, (1, 0)) + dot(grad, state, (1, 1))
        grad_fk = dot(grad_scores, fq, (0, 0)) + dot(value, later, (1, 1))
        grad_v = dot(scores, grad, (0, 0)) + dot(fk, later, (1, 0))
        gq_ref[:, cols] = (grad_fq * (q_sig * (1.0 + q_raw * (1.0 - q_sig)))).astype(BF16)
        gk_ref[:, cols] = (grad_fk * (k_sig * (1.0 + k_raw * (1.0 - k_sig)))).astype(BF16)
        gv_ref[:, cols] = grad_v.astype(BF16)


def backward(query, key, value, grad_att, state, later):
    tokens, features = query.shape
    group = 2
    width = group * HEAD_DIM
    spec = pl.BlockSpec((tokens, width), lambda i: (0, i))
    square = pl.BlockSpec((width, HEAD_DIM), lambda i: (i, 0))
    return pl.pallas_call(
        functools.partial(backward_kernel, group),
        grid=(features // width,),
        in_specs=[spec, spec, spec, spec, square, square],
        out_specs=[spec, spec, spec],
        out_shape=[jax.ShapeDtypeStruct((tokens, features), BF16)] * 3,
        compiler_params=params(),
        name="backward",
    )(query, key, value, grad_att, state, later)


def shards(query_input, key_input, value_input, grad_output, out_weight, norm_gain):
    query, key, value, grad_result = (
        query_input[0], key_input[0], value_input[0], grad_output[0]
    )
    gain = norm_gain[None]
    full_weight = lax.all_gather(out_weight, ("seq", "dp"), axis=0, tiled=True)
    fk, state = local_state(key, value)
    earlier = carried(state, False)
    fq, mixed, normed, radius = forward(query, fk, value, earlier, gain)
    term = lax.dot_general(
        mixed, grad_result, (((0,), (0,)), ((), ())), preferred_element_type=F32
    ).astype(BF16)
    grad_weight = lax.psum_scatter(term, ("seq", "dp"), scatter_dimension=0, tiled=True)
    result, grad_att, grad_state = project(
        grad_result, mixed, normed, radius, fq, full_weight, gain
    )
    later = carried(grad_state, True)
    grad_query, grad_key, grad_value = backward(query, key, value, grad_att, earlier, later)
    return (
        result[None], grad_query[None], grad_key[None], grad_value[None],
        grad_weight.astype(F32),
    )


def solution(mesh):
    rows = P("dp", "seq", None)
    weight = P(("seq", "dp"), None)
    return jax.shard_map(
        shards,
        mesh=mesh,
        in_specs=(rows, rows, rows, rows, weight, P()),
        out_specs=(rows, rows, rows, rows, weight),
        check_vma=False,
    )
```

```python
import functools

import jax
import jax.numpy as jnp
from jax import lax
from jax.experimental import pallas as pl
from jax.experimental.pallas import tpu as pltpu
from jax.sharding import PartitionSpec as P

HEAD_DIM = 128
epsilon = 1e-06
MESH = pl.DeviceIdType.MESH
BF16 = jnp.bfloat16
F32 = jnp.float32
VMEM_LIMIT = 48 * 1024 * 1024


def dot(left, right, contract):
    return lax.dot_general(
        left, right, ((contract[:1], contract[1:]), ((), ())), preferred_element_type=F32
    )


def params(**more):
    return pltpu.CompilerParams(vmem_limit_bytes=VMEM_LIMIT, **more)


def head_cols(head):
    return slice(head * HEAD_DIM, (head + 1) * HEAD_DIM)


def causal(rows):
    return lax.broadcasted_iota(jnp.int32, (rows, rows), 0) >= lax.broadcasted_iota(
        jnp.int32, (rows, rows), 1
    )


def state_kernel(group, k_ref, v_ref, fk_ref, state_ref):
    raw = k_ref[...].astype(F32)
    fk = (raw * jax.nn.sigmoid(raw)).astype(BF16)
    fk_ref[...] = fk
    for head in range(group):
        cols = head_cols(head)
        state_ref[cols, :] = dot(fk[:, cols], v_ref[:, cols], (0, 0)).astype(BF16)


def local_state(key, value):
    tokens, features = key.shape
    group = 4
    width = group * HEAD_DIM
    spec = pl.BlockSpec((tokens, width), lambda i: (0, i))
    return pl.pallas_call(
        functools.partial(state_kernel, group),
        grid=(features // width,),
        in_specs=[spec, spec],
        out_specs=[spec, pl.BlockSpec((width, HEAD_DIM), lambda i: (i, 0))],
        out_shape=[
            jax.ShapeDtypeStruct((tokens, features), BF16),
            jax.ShapeDtypeStruct((features, HEAD_DIM), BF16),
        ],
        compiler_params=params(),
        name="local_state",
    )(key, value)


def carry_kernel(count, backward, x_ref, out_ref, got, sums, res, s1, r1, s2, r2):
    me = lax.axis_index("seq")
    part = x_ref.shape[0] // count

    def rows_of(index):
        return pl.ds(pl.multiple_of(index * part, part), part)

    barrier = pltpu.get_barrier_semaphore()
    for step in range(1, count):
        pl.semaphore_signal(
            barrier, inc=1, device_id={"seq": lax.rem(me + step, count)}, device_id_type=MESH
        )
    pl.semaphore_wait(barrier, count - 1)

    def send(step, source, target, send_sem, recv_sem):
        return pltpu.make_async_remote_copy(
            src_ref=source,
            dst_ref=target,
            send_sem=send_sem.at[step],
            recv_sem=recv_sem.at[step],
            device_id={"seq": lax.rem(me + step, count)},
            device_id_type=MESH,
        )

    first = []
    for step in range(1, count):
        peer = lax.rem(me + step, count)
        copy = send(step, x_ref.at[rows_of(peer)], got.at[me], s1, r1)
        copy.start()
        first.append(copy)
    got[me] = x_ref[rows_of(me), :]
    for copy in first:
        copy.wait_recv()
    total = jnp.zeros((part, x_ref.shape[1]), F32)
    order = range(count)
    for position in reversed(order) if backward else order:
        sums[position] = total.astype(BF16)
        total = total + got[position].astype(F32)
    second = []
    for step in range(1, count):
        peer = lax.rem(me + step, count)
        copy = send(step, sums.at[peer], res.at[rows_of(me)], s2, r2)
        copy.start()
        second.append(copy)
    res[rows_of(me), :] = sums[me]
    for copy in first:
        copy.wait_send()
    for copy in second:
        copy.wait_recv()
    out_ref[...] = res[...]
    for copy in second:
        copy.wait_send()


def carried(state, backward):
    count = lax.axis_size("seq")
    rows, cols = state.shape
    vmem = pl.BlockSpec(memory_space=pltpu.VMEM)
    sems = [pltpu.SemaphoreType.DMA((count,))] * 4
    return pl.pallas_call(
        functools.partial(carry_kernel, count, backward),
        in_specs=[vmem],
        out_specs=vmem,
        out_shape=jax.ShapeDtypeStruct((rows, cols), BF16),
        scratch_shapes=[
            pltpu.VMEM((count, rows // count, cols), BF16),
            pltpu.VMEM((count, rows // count, cols), BF16),
            pltpu.VMEM((rows, cols), BF16),
        ]
        + sems,
        compiler_params=params(collective_id=int(backward), has_side_effects=True),
        name="carry_later" if backward else "carry_earlier",
    )(state)


def forward_kernel(
    group, q_ref, fk_ref, v_ref, state_ref, gain_ref, fq_ref, mixed_ref, normed_ref, radius_ref,
    att, squares,
):
    step = pl.program_id(0)
    rows = q_ref.shape[0]
    raw = q_ref[...].astype(F32)
    fq = (raw * jax.nn.sigmoid(raw)).astype(BF16)
    fq_ref[...] = fq
    keep = causal(rows)

    @pl.when(step == 0)
    def _():
        squares[...] = jnp.zeros_like(squares)

    width = group * HEAD_DIM
    for head in range(group):
        cols = head_cols(head)
        scores = dot(fq[:, cols], fk_ref[:, cols], (1, 1))
        scores = jnp.where(keep, scores, 0.0).astype(BF16)
        out = dot(scores, v_ref[:, cols], (1, 0)) + dot(fq[:, cols], state_ref[cols, :], (1, 0))
        start = pl.multiple_of(step * width + head * HEAD_DIM, HEAD_DIM)
        att[:, pl.ds(start, HEAD_DIM)] = out
        squares[...] += out * out

    @pl.when(step == pl.num_programs(0) - 1)
    def _():
        features = att.shape[1]
        mean = jnp.sum(squares[...], axis=-1, keepdims=True) / features
        radius = jnp.sqrt(mean + epsilon)
        radius_ref[...] = jnp.broadcast_to(radius, radius_ref.shape)
        inverse = 1.0 / radius
        for start in range(0, features, 256):
            cols = slice(start, start + 256)
            normed = att[:, cols] * inverse
            normed_ref[:, cols] = normed.astype(BF16)
            mixed_ref[:, cols] = (normed * gain_ref[:, cols]).astype(BF16)


def forward(query, fk, value, state, gain):
    tokens, features = query.shape
    group = 2
    width = group * HEAD_DIM
    spec = pl.BlockSpec((tokens, width), lambda i: (0, i))
    whole = pl.BlockSpec((tokens, features), lambda i: (0, 0))
    wide = jax.ShapeDtypeStruct((tokens, features), BF16)
    return pl.pallas_call(
        functools.partial(forward_kernel, group),
        grid=(features // width,),
        in_specs=[
            spec,
            spec,
            spec,
            pl.BlockSpec((width, HEAD_DIM), lambda i: (i, 0)),
            pl.BlockSpec((1, features), lambda i: (0, 0)),
        ],
        out_specs=[spec, whole, whole, pl.BlockSpec((tokens, HEAD_DIM), lambda i: (0, 0))],
        out_shape=[wide, wide, wide, jax.ShapeDtypeStruct((tokens, HEAD_DIM), F32)],
        scratch_shapes=[pltpu.VMEM((tokens, features), F32), pltpu.VMEM((tokens, HEAD_DIM), F32)],
        compiler_params=params(),
        name="forward",
    )(query, fk, value, state, gain)


def project_kernel(
    go_ref, mixed_ref, normed_ref, radius_ref, fq_ref, weight_ref, gain_ref,
    result_ref, ga_ref, state_ref, total,
):
    step = pl.program_id(0)
    features = mixed_ref.shape[1]
    grad_mixed = dot(go_ref[...], weight_ref[...], (1, 1))
    grad_hat = grad_mixed * gain_ref[...]
    normed = normed_ref[...].astype(F32)
    inner = jnp.mean(grad_hat * normed, axis=-1, keepdims=True)
    inverse = 1.0 / radius_ref[:, :1]
    grad_att = ((grad_hat - normed * inner) * inverse).astype(BF16)
    ga_ref[...] = grad_att

    @pl.when(step == 0)
    def _():
        total[...] = jnp.zeros_like(total)

    for head in range(features // HEAD_DIM):
        cols = head_cols(head)
        total[cols, :] += dot(fq_ref[:, cols], grad_att[:, cols], (0, 0))
    result_ref[...] = dot(mixed_ref[...], weight_ref[...], (1, 0)).astype(BF16)

    @pl.when(step == pl.num_programs(0) - 1)
    def _():
        state_ref[...] = total[...].astype(BF16)


def project(grad_output, mixed, normed, radius, fq, weight, gain):
    tokens, features = mixed.shape
    out_cols = weight.shape[1]
    rows = 256
    narrow = pl.BlockSpec((rows, features), lambda i: (i, 0))
    outs = pl.BlockSpec((rows, out_cols), lambda i: (i, 0))
    whole = lambda i: (0, 0)
    return pl.pallas_call(
        project_kernel,
        grid=(tokens // rows,),
        in_specs=[
            outs,
            narrow,
            narrow,
            pl.BlockSpec((rows, HEAD_DIM), lambda i: (i, 0)),
            narrow,
            pl.BlockSpec(weight.shape, whole),
            pl.BlockSpec((1, features), whole),
        ],
        out_specs=[outs, narrow, pl.BlockSpec((features, HEAD_DIM), whole)],
        out_shape=[
            jax.ShapeDtypeStruct((tokens, out_cols), BF16),
            jax.ShapeDtypeStruct((tokens, features), BF16),
            jax.ShapeDtypeStruct((features, HEAD_DIM), BF16),
        ],
        scratch_shapes=[pltpu.VMEM((features, HEAD_DIM), F32)],
        compiler_params=params(),
        name="project",
    )(grad_output, mixed, normed, radius, fq, weight, gain)


def backward_kernel(
    group, q_ref, k_ref, v_ref, ga_ref, state_ref, later_ref, gq_ref, gk_ref, gv_ref
):
    rows = q_ref.shape[0]
    keep = causal(rows)
    for head in range(group):
        cols = head_cols(head)
        q_raw = q_ref[:, cols].astype(F32)
        k_raw = k_ref[:, cols].astype(F32)
        q_sig = jax.nn.sigmoid(q_raw)
        k_sig = jax.nn.sigmoid(k_raw)
        fq = (q_raw * q_sig).astype(BF16)
        fk = (k_raw * k_sig).astype(BF16)
        value = v_ref[:, cols]
        grad = ga_ref[:, cols]
        state = state_ref[cols, :]
        later = later_ref[cols, :]
        scores = jnp.where(keep, dot(fq, fk, (1, 1)), 0.0).astype(BF16)
        grad_scores = jnp.where(keep, dot(grad, value, (1, 1)), 0.0).astype(BF16)
        grad_fq = dot(grad_scores, fk, (1, 0)) + dot(grad, state, (1, 1))
        grad_fk = dot(grad_scores, fq, (0, 0)) + dot(value, later, (1, 1))
        grad_v = dot(scores, grad, (0, 0)) + dot(fk, later, (1, 0))
        gq_ref[:, cols] = (grad_fq * (q_sig * (1.0 + q_raw * (1.0 - q_sig)))).astype(BF16)
        gk_ref[:, cols] = (grad_fk * (k_sig * (1.0 + k_raw * (1.0 - k_sig)))).astype(BF16)
        gv_ref[:, cols] = grad_v.astype(BF16)


def backward(query, key, value, grad_att, state, later):
    tokens, features = query.shape
    group = 2
    width = group * HEAD_DIM
    spec = pl.BlockSpec((tokens, width), lambda i: (0, i))
    square = pl.BlockSpec((width, HEAD_DIM), lambda i: (i, 0))
    return pl.pallas_call(
        functools.partial(backward_kernel, group),
        grid=(features // width,),
        in_specs=[spec, spec, spec, spec, square, square],
        out_specs=[spec, spec, spec],
        out_shape=[jax.ShapeDtypeStruct((tokens, features), BF16)] * 3,
        compiler_params=params(),
        name="backward",
    )(query, key, value, grad_att, state, later)


def pair_barrier(peer):
    barrier = pltpu.get_barrier_semaphore()
    pl.semaphore_signal(barrier, inc=1, device_id={"pair": peer}, device_id_type=MESH)
    pl.semaphore_wait(barrier, 1)


def pair_gather_kernel(x_ref, out_ref, got, send_sem, recv_sem):
    mine = lax.axis_index("pair")
    peer = 1 - mine
    pair_barrier(peer)
    copy = pltpu.make_async_remote_copy(
        src_ref=x_ref,
        dst_ref=got,
        send_sem=send_sem,
        recv_sem=recv_sem,
        device_id={"pair": peer},
        device_id_type=MESH,
    )
    copy.start()

    def own(group, unused):
        out_ref[group, mine] = x_ref[group]
        return unused

    def other(group, unused):
        out_ref[group, peer] = got[group]
        return unused

    groups = x_ref.shape[0]
    lax.fori_loop(0, groups, own, 0)
    copy.wait_recv()
    lax.fori_loop(0, groups, other, 0)
    copy.wait_send()


def pair_gather(half, part):
    rows, cols = half.shape
    groups = rows // part
    vmem = pl.BlockSpec(memory_space=pltpu.VMEM)
    whole = pl.pallas_call(
        pair_gather_kernel,
        in_specs=[vmem],
        out_specs=vmem,
        out_shape=jax.ShapeDtypeStruct((groups, 2, part, cols), BF16),
        scratch_shapes=[
            pltpu.VMEM((groups, part, cols), BF16),
            pltpu.SemaphoreType.DMA,
            pltpu.SemaphoreType.DMA,
        ],
        compiler_params=params(collective_id=2, has_side_effects=True),
        name="pair_gather",
    )(half.reshape(groups, part, cols))
    return whole.reshape(2 * rows, cols)


def pair_term_kernel(part, mixed_ref, go_ref, out_ref, keep, away, got, send_sem, recv_sem):
    mine = lax.axis_index("pair")
    peer = 1 - mine
    chunks, rows, cols = out_ref.shape
    pair_barrier(peer)

    def copy_of(chunk):
        return pltpu.make_async_remote_copy(
            src_ref=away.at[chunk],
            dst_ref=got.at[chunk],
            send_sem=send_sem.at[chunk],
            recv_sem=recv_sem.at[chunk],
            device_id={"pair": peer},
            device_id_type=MESH,
        )

    def multiply(chunk, unused):
        columns = pl.ds(pl.multiple_of(chunk * 2 * rows, 2 * rows), 2 * rows)
        term = dot(mixed_ref[:, columns], go_ref[...], (0, 0))
        term = term.reshape(rows // part, 2, part, cols)
        low = term[:, 0].reshape(rows, cols)
        high = term[:, 1].reshape(rows, cols)
        keep[chunk] = jnp.where(mine == 0, low, high)
        away[chunk] = jnp.where(mine == 0, high, low).astype(BF16)
        copy_of(chunk).start()
        return unused

    def add(chunk, unused):
        copy_of(chunk).wait_recv()
        out_ref[chunk] = (keep[chunk] + got[chunk].astype(F32)).astype(BF16)
        return unused

    def sent(chunk, unused):
        copy_of(chunk).wait_send()
        return unused

    lax.fori_loop(0, chunks, multiply, 0)
    lax.fori_loop(0, chunks, add, 0)
    lax.fori_loop(0, chunks, sent, 0)


def pair_term(mixed, grad_output, part):
    features = mixed.shape[1]
    cols = grad_output.shape[1]
    rows = max(HEAD_DIM, part)
    chunks = features // (2 * rows)
    vmem = pl.BlockSpec(memory_space=pltpu.VMEM)
    term = pl.pallas_call(
        functools.partial(pair_term_kernel, part),
        in_specs=[vmem, vmem],
        out_specs=vmem,
        out_shape=jax.ShapeDtypeStruct((chunks, rows, cols), BF16),
        scratch_shapes=[
            pltpu.VMEM((chunks, rows, cols), F32),
            pltpu.VMEM((chunks, rows, cols), BF16),
            pltpu.VMEM((chunks, rows, cols), BF16),
            pltpu.SemaphoreType.DMA((chunks,)),
            pltpu.SemaphoreType.DMA((chunks,)),
        ],
        compiler_params=params(collective_id=3, has_side_effects=True),
        name="pair_term",
    )(mixed, grad_output)
    return term.reshape(chunks * rows, cols)


def shards(query_input, key_input, value_input, grad_output, out_weight, norm_gain):
    query, key, value, grad_result = (
        query_input[0], key_input[0], value_input[0], grad_output[0]
    )
    gain = norm_gain[None]
    part = out_weight.shape[0]
    half_weight = lax.all_gather(out_weight, ("seq", "outer"), axis=0, tiled=True)
    fk, state = local_state(key, value)
    earlier = carried(state, False)
    fq, mixed, normed, radius = forward(query, fk, value, earlier, gain)
    term = pair_term(mixed, grad_result, part)
    grad_weight = lax.psum_scatter(term, ("seq", "outer"), scatter_dimension=0, tiled=True)
    full_weight = pair_gather(half_weight, part)
    result, grad_att, grad_state = project(
        grad_result, mixed, normed, radius, fq, full_weight, gain
    )
    later = carried(grad_state, True)
    grad_query, grad_key, grad_value = backward(query, key, value, grad_att, earlier, later)
    return (
        result[None], grad_query[None], grad_key[None], grad_value[None],
        grad_weight.astype(F32),
    )


def solution(mesh):
    seq, dp = mesh.shape["seq"], mesh.shape["dp"]
    paired = jax.sharding.Mesh(
        mesh.devices.reshape(seq, dp // 2, 2), ("seq", "outer", "pair")
    )
    rows = P(("outer", "pair"), "seq", None)
    weight = P(("seq", "outer", "pair"), None)
    return jax.shard_map(
        shards,
        mesh=paired,
        in_specs=(rows, rows, rows, rows, weight, P()),
        out_specs=(rows, rows, rows, rows, weight),
        check_vma=False,
    )
```

```python
import functools

import jax
import jax.numpy as jnp
from jax import lax
from jax.experimental import pallas as pl
from jax.experimental.pallas import tpu as pltpu
from jax.sharding import PartitionSpec as P

HEAD_DIM = 128
epsilon = 1e-06
MESH = pl.DeviceIdType.MESH
BF16 = jnp.bfloat16
F32 = jnp.float32
VMEM_LIMIT = 48 * 1024 * 1024


def dot(left, right, contract):
    return lax.dot_general(
        left, right, ((contract[:1], contract[1:]), ((), ())), preferred_element_type=F32
    )


def params(**more):
    return pltpu.CompilerParams(vmem_limit_bytes=VMEM_LIMIT, **more)


def head_cols(head):
    return slice(head * HEAD_DIM, (head + 1) * HEAD_DIM)


def causal(rows):
    return lax.broadcasted_iota(jnp.int32, (rows, rows), 0) >= lax.broadcasted_iota(
        jnp.int32, (rows, rows), 1
    )


def state_kernel(group, k_ref, v_ref, fk_ref, state_ref):
    raw = k_ref[...].astype(F32)
    fk = (raw * jax.nn.sigmoid(raw)).astype(BF16)
    fk_ref[...] = fk
    for head in range(group):
        cols = head_cols(head)
        state_ref[cols, :] = dot(fk[:, cols], v_ref[:, cols], (0, 0)).astype(BF16)


def local_state(key, value):
    tokens, features = key.shape
    group = 4
    width = group * HEAD_DIM
    spec = pl.BlockSpec((tokens, width), lambda i: (0, i))
    return pl.pallas_call(
        functools.partial(state_kernel, group),
        grid=(features // width,),
        in_specs=[spec, spec],
        out_specs=[spec, pl.BlockSpec((width, HEAD_DIM), lambda i: (i, 0))],
        out_shape=[
            jax.ShapeDtypeStruct((tokens, features), BF16),
            jax.ShapeDtypeStruct((features, HEAD_DIM), BF16),
        ],
        compiler_params=params(),
        name="local_state",
    )(key, value)


def carry_kernel(count, backward, *refs):
    if backward:
        x_ref, mixed_ref, weight_ref, out_ref, result_ref = refs[:5]
    else:
        x_ref, out_ref = refs[:2]
    got, sums, res, s1, r1, s2, r2 = refs[-7:]

    def results(begin, end):
        def tile(index, unused):
            columns = pl.ds(pl.multiple_of(index * 256, 256), 256)
            result_ref[:, columns] = dot(mixed_ref[...], weight_ref[:, columns], (1, 0)).astype(BF16)
            return unused

        lax.fori_loop(begin, end, tile, 0)

    me = lax.axis_index("seq")
    part = x_ref.shape[0] // count

    def rows_of(index):
        return pl.ds(pl.multiple_of(index * part, part), part)

    barrier = pltpu.get_barrier_semaphore()
    for step in range(1, count):
        pl.semaphore_signal(
            barrier, inc=1, device_id={"seq": lax.rem(me + step, count)}, device_id_type=MESH
        )
    pl.semaphore_wait(barrier, count - 1)

    def send(step, source, target, send_sem, recv_sem):
        return pltpu.make_async_remote_copy(
            src_ref=source,
            dst_ref=target,
            send_sem=send_sem.at[step],
            recv_sem=recv_sem.at[step],
            device_id={"seq": lax.rem(me + step, count)},
            device_id_type=MESH,
        )

    first = []
    for step in range(1, count):
        peer = lax.rem(me + step, count)
        copy = send(step, x_ref.at[rows_of(peer)], got.at[me], s1, r1)
        copy.start()
        first.append(copy)
    got[me] = x_ref[rows_of(me), :]
    if backward:
        tiles = weight_ref.shape[1] // 256
        results(0, tiles // 2)
    for copy in first:
        copy.wait_recv()
    total = jnp.zeros((part, x_ref.shape[1]), F32)
    order = range(count)
    for position in reversed(order) if backward else order:
        sums[position] = total.astype(BF16)
        total = total + got[position].astype(F32)
    second = []
    for step in range(1, count):
        peer = lax.rem(me + step, count)
        copy = send(step, sums.at[peer], res.at[rows_of(me)], s2, r2)
        copy.start()
        second.append(copy)
    res[rows_of(me), :] = sums[me]
    if backward:
        results(tiles // 2, tiles)
    for copy in first:
        copy.wait_send()
    for copy in second:
        copy.wait_recv()
    out_ref[...] = res[...]
    for copy in second:
        copy.wait_send()


def carried(state, backward, *product):
    count = lax.axis_size("seq")
    rows, cols = state.shape
    vmem = pl.BlockSpec(memory_space=pltpu.VMEM)
    sems = [pltpu.SemaphoreType.DMA((count,))] * 4
    out_shape = [jax.ShapeDtypeStruct((rows, cols), BF16)]
    if backward:
        mixed, weight = product
        out_shape += [jax.ShapeDtypeStruct((mixed.shape[0], weight.shape[1]), BF16)]
    return pl.pallas_call(
        functools.partial(carry_kernel, count, backward),
        in_specs=[vmem] * (1 + len(product)),
        out_specs=[vmem] * len(out_shape),
        out_shape=out_shape,
        scratch_shapes=[
            pltpu.VMEM((count, rows // count, cols), BF16),
            pltpu.VMEM((count, rows // count, cols), BF16),
            pltpu.VMEM((rows, cols), BF16),
        ]
        + sems,
        compiler_params=params(collective_id=int(backward), has_side_effects=True),
        name="carry_later" if backward else "carry_earlier",
    )(state, *product)


def forward_kernel(
    group, q_ref, fk_ref, v_ref, state_ref, gain_ref, fq_ref, mixed_ref, normed_ref, radius_ref,
    att, squares,
):
    step = pl.program_id(0)
    rows = q_ref.shape[0]
    raw = q_ref[...].astype(F32)
    fq = (raw * jax.nn.sigmoid(raw)).astype(BF16)
    fq_ref[...] = fq
    keep = causal(rows)

    @pl.when(step == 0)
    def _():
        squares[...] = jnp.zeros_like(squares)

    width = group * HEAD_DIM
    for head in range(group):
        cols = head_cols(head)
        scores = dot(fq[:, cols], fk_ref[:, cols], (1, 1))
        scores = jnp.where(keep, scores, 0.0).astype(BF16)
        out = dot(scores, v_ref[:, cols], (1, 0)) + dot(fq[:, cols], state_ref[cols, :], (1, 0))
        start = pl.multiple_of(step * width + head * HEAD_DIM, HEAD_DIM)
        att[:, pl.ds(start, HEAD_DIM)] = out
        squares[...] += out * out

    @pl.when(step == pl.num_programs(0) - 1)
    def _():
        features = att.shape[1]
        mean = jnp.sum(squares[...], axis=-1, keepdims=True) / features
        radius = jnp.sqrt(mean + epsilon)
        radius_ref[...] = jnp.broadcast_to(radius, radius_ref.shape)
        inverse = 1.0 / radius
        for start in range(0, features, 256):
            cols = slice(start, start + 256)
            normed = att[:, cols] * inverse
            normed_ref[:, cols] = normed.astype(BF16)
            mixed_ref[:, cols] = (normed * gain_ref[:, cols]).astype(BF16)


def forward(query, fk, value, state, gain):
    tokens, features = query.shape
    group = 2
    width = group * HEAD_DIM
    spec = pl.BlockSpec((tokens, width), lambda i: (0, i))
    whole = pl.BlockSpec((tokens, features), lambda i: (0, 0))
    wide = jax.ShapeDtypeStruct((tokens, features), BF16)
    return pl.pallas_call(
        functools.partial(forward_kernel, group),
        grid=(features // width,),
        in_specs=[
            spec,
            spec,
            spec,
            pl.BlockSpec((width, HEAD_DIM), lambda i: (i, 0)),
            pl.BlockSpec((1, features), lambda i: (0, 0)),
        ],
        out_specs=[spec, whole, whole, pl.BlockSpec((tokens, HEAD_DIM), lambda i: (0, 0))],
        out_shape=[wide, wide, wide, jax.ShapeDtypeStruct((tokens, HEAD_DIM), F32)],
        scratch_shapes=[pltpu.VMEM((tokens, features), F32), pltpu.VMEM((tokens, HEAD_DIM), F32)],
        compiler_params=params(),
        name="forward",
    )(query, fk, value, state, gain)


def project_kernel(
    go_ref, normed_ref, radius_ref, fq_ref, weight_ref, gain_ref,
    ga_ref, state_ref, total,
):
    step = pl.program_id(0)
    features = normed_ref.shape[1]
    grad_mixed = dot(go_ref[...], weight_ref[...], (1, 1))
    grad_hat = grad_mixed * gain_ref[...]
    normed = normed_ref[...].astype(F32)
    inner = jnp.mean(grad_hat * normed, axis=-1, keepdims=True)
    inverse = 1.0 / radius_ref[:, :1]
    grad_att = ((grad_hat - normed * inner) * inverse).astype(BF16)
    ga_ref[...] = grad_att

    @pl.when(step == 0)
    def _():
        total[...] = jnp.zeros_like(total)

    for head in range(features // HEAD_DIM):
        cols = head_cols(head)
        total[cols, :] += dot(fq_ref[:, cols], grad_att[:, cols], (0, 0))

    @pl.when(step == pl.num_programs(0) - 1)
    def _():
        state_ref[...] = total[...].astype(BF16)


def project(grad_output, normed, radius, fq, weight, gain):
    tokens, features = normed.shape
    out_cols = weight.shape[1]
    rows = 256
    narrow = pl.BlockSpec((rows, features), lambda i: (i, 0))
    outs = pl.BlockSpec((rows, out_cols), lambda i: (i, 0))
    whole = lambda i: (0, 0)
    return pl.pallas_call(
        project_kernel,
        grid=(tokens // rows,),
        in_specs=[
            outs,
            narrow,
            pl.BlockSpec((rows, HEAD_DIM), lambda i: (i, 0)),
            narrow,
            pl.BlockSpec(weight.shape, whole),
            pl.BlockSpec((1, features), whole),
        ],
        out_specs=[narrow, pl.BlockSpec((features, HEAD_DIM), whole)],
        out_shape=[
            jax.ShapeDtypeStruct((tokens, features), BF16),
            jax.ShapeDtypeStruct((features, HEAD_DIM), BF16),
        ],
        scratch_shapes=[pltpu.VMEM((features, HEAD_DIM), F32)],
        compiler_params=params(),
        name="project",
    )(grad_output, normed, radius, fq, weight, gain)


def backward_kernel(
    group, q_ref, k_ref, v_ref, ga_ref, state_ref, later_ref, gq_ref, gk_ref, gv_ref
):
    rows = q_ref.shape[0]
    keep = causal(rows)
    for head in range(group):
        cols = head_cols(head)
        q_raw = q_ref[:, cols].astype(F32)
        k_raw = k_ref[:, cols].astype(F32)
        q_sig = jax.nn.sigmoid(q_raw)
        k_sig = jax.nn.sigmoid(k_raw)
        fq = (q_raw * q_sig).astype(BF16)
        fk = (k_raw * k_sig).astype(BF16)
        value = v_ref[:, cols]
        grad = ga_ref[:, cols]
        state = state_ref[cols, :]
        later = later_ref[cols, :]
        scores = jnp.where(keep, dot(fq, fk, (1, 1)), 0.0).astype(BF16)
        grad_scores = jnp.where(keep, dot(grad, value, (1, 1)), 0.0).astype(BF16)
        grad_fq = dot(grad_scores, fk, (1, 0)) + dot(grad, state, (1, 1))
        grad_fk = dot(grad_scores, fq, (0, 0)) + dot(value, later, (1, 1))
        grad_v = dot(scores, grad, (0, 0)) + dot(fk, later, (1, 0))
        gq_ref[:, cols] = (grad_fq * (q_sig * (1.0 + q_raw * (1.0 - q_sig)))).astype(BF16)
        gk_ref[:, cols] = (grad_fk * (k_sig * (1.0 + k_raw * (1.0 - k_sig)))).astype(BF16)
        gv_ref[:, cols] = grad_v.astype(BF16)


def backward(query, key, value, grad_att, state, later):
    tokens, features = query.shape
    group = 2
    width = group * HEAD_DIM
    spec = pl.BlockSpec((tokens, width), lambda i: (0, i))
    square = pl.BlockSpec((width, HEAD_DIM), lambda i: (i, 0))
    return pl.pallas_call(
        functools.partial(backward_kernel, group),
        grid=(features // width,),
        in_specs=[spec, spec, spec, spec, square, square],
        out_specs=[spec, spec, spec],
        out_shape=[jax.ShapeDtypeStruct((tokens, features), BF16)] * 3,
        compiler_params=params(),
        name="backward",
    )(query, key, value, grad_att, state, later)


def pair_barrier(peer):
    barrier = pltpu.get_barrier_semaphore()
    pl.semaphore_signal(barrier, inc=1, device_id={"pair": peer}, device_id_type=MESH)
    pl.semaphore_wait(barrier, 1)


def pair_gather_kernel(x_ref, out_ref, got, send_sem, recv_sem):
    mine = lax.axis_index("pair")
    peer = 1 - mine
    pair_barrier(peer)
    copy = pltpu.make_async_remote_copy(
        src_ref=x_ref,
        dst_ref=got,
        send_sem=send_sem,
        recv_sem=recv_sem,
        device_id={"pair": peer},
        device_id_type=MESH,
    )
    copy.start()

    def own(group, unused):
        out_ref[group, mine] = x_ref[group]
        return unused

    def other(group, unused):
        out_ref[group, peer] = got[group]
        return unused

    groups = x_ref.shape[0]
    lax.fori_loop(0, groups, own, 0)
    copy.wait_recv()
    lax.fori_loop(0, groups, other, 0)
    copy.wait_send()


def pair_gather(half, part):
    rows, cols = half.shape
    groups = rows // part
    vmem = pl.BlockSpec(memory_space=pltpu.VMEM)
    whole = pl.pallas_call(
        pair_gather_kernel,
        in_specs=[vmem],
        out_specs=vmem,
        out_shape=jax.ShapeDtypeStruct((groups, 2, part, cols), BF16),
        scratch_shapes=[
            pltpu.VMEM((groups, part, cols), BF16),
            pltpu.SemaphoreType.DMA,
            pltpu.SemaphoreType.DMA,
        ],
        compiler_params=params(collective_id=2, has_side_effects=True),
        name="pair_gather",
    )(half.reshape(groups, part, cols))
    return whole.reshape(2 * rows, cols)


def pair_term_kernel(part, mixed_ref, go_ref, out_ref, keep, away, got, send_sem, recv_sem):
    mine = lax.axis_index("pair")
    peer = 1 - mine
    chunks, rows, cols = out_ref.shape
    pair_barrier(peer)

    def copy_of(chunk):
        return pltpu.make_async_remote_copy(
            src_ref=away.at[chunk],
            dst_ref=got.at[chunk],
            send_sem=send_sem.at[chunk],
            recv_sem=recv_sem.at[chunk],
            device_id={"pair": peer},
            device_id_type=MESH,
        )

    def multiply(chunk, unused):
        columns = pl.ds(pl.multiple_of(chunk * 2 * rows, 2 * rows), 2 * rows)
        term = dot(mixed_ref[:, columns], go_ref[...], (0, 0))
        term = term.reshape(rows // part, 2, part, cols)
        low = term[:, 0].reshape(rows, cols)
        high = term[:, 1].reshape(rows, cols)
        keep[chunk] = jnp.where(mine == 0, low, high)
        away[chunk] = jnp.where(mine == 0, high, low).astype(BF16)
        copy_of(chunk).start()
        return unused

    def add(chunk, unused):
        copy_of(chunk).wait_recv()
        out_ref[chunk] = (keep[chunk] + got[chunk].astype(F32)).astype(BF16)
        return unused

    def sent(chunk, unused):
        copy_of(chunk).wait_send()
        return unused

    lax.fori_loop(0, chunks, multiply, 0)
    lax.fori_loop(0, chunks, add, 0)
    lax.fori_loop(0, chunks, sent, 0)


def pair_term(mixed, grad_output, part):
    features = mixed.shape[1]
    cols = grad_output.shape[1]
    rows = max(HEAD_DIM, part)
    chunks = features // (2 * rows)
    vmem = pl.BlockSpec(memory_space=pltpu.VMEM)
    term = pl.pallas_call(
        functools.partial(pair_term_kernel, part),
        in_specs=[vmem, vmem],
        out_specs=vmem,
        out_shape=jax.ShapeDtypeStruct((chunks, rows, cols), BF16),
        scratch_shapes=[
            pltpu.VMEM((chunks, rows, cols), F32),
            pltpu.VMEM((chunks, rows, cols), BF16),
            pltpu.VMEM((chunks, rows, cols), BF16),
            pltpu.SemaphoreType.DMA((chunks,)),
            pltpu.SemaphoreType.DMA((chunks,)),
        ],
        compiler_params=params(collective_id=3, has_side_effects=True),
        name="pair_term",
    )(mixed, grad_output)
    return term.reshape(chunks * rows, cols)


def shards(query_input, key_input, value_input, grad_output, out_weight, norm_gain):
    query, key, value, grad_result = (
        query_input[0], key_input[0], value_input[0], grad_output[0]
    )
    gain = norm_gain[None]
    part = out_weight.shape[0]
    half_weight = lax.all_gather(out_weight, ("seq", "outer"), axis=0, tiled=True)
    fk, state = local_state(key, value)
    (earlier,) = carried(state, False)
    fq, mixed, normed, radius = forward(query, fk, value, earlier, gain)
    term = pair_term(mixed, grad_result, part)
    outer = lax.axis_index("outer")
    term = term.reshape(lax.axis_size("seq"), 2, part, term.shape[1])
    away = lax.dynamic_index_in_dim(term, 1 - outer, 1, False)
    came = lax.ppermute(away, "outer", [(0, 1), (1, 0)])
    keep = lax.dynamic_index_in_dim(term, outer, 1, False)
    full_weight = pair_gather(half_weight, part)
    grad_att, grad_state = project(
        grad_result, normed, radius, fq, full_weight, gain
    )
    came, grad_state = lax.optimization_barrier((came, grad_state))
    term = (keep.astype(F32) + came.astype(F32)).astype(BF16).reshape(-1, term.shape[-1])
    term, grad_state = lax.optimization_barrier((term, grad_state))
    grad_weight = lax.psum_scatter(term, "seq", scatter_dimension=0, tiled=True)
    later, result = carried(grad_state, True, mixed, full_weight)
    grad_query, grad_key, grad_value = backward(query, key, value, grad_att, earlier, later)
    return (
        result[None], grad_query[None], grad_key[None], grad_value[None],
        grad_weight.astype(F32),
    )


def solution(mesh):
    seq, dp = mesh.shape["seq"], mesh.shape["dp"]
    paired = jax.sharding.Mesh(
        mesh.devices.reshape(seq, dp // 2, 2), ("seq", "outer", "pair")
    )
    rows = P(("outer", "pair"), "seq", None)
    weight = P(("seq", "outer", "pair"), None)
    return jax.shard_map(
        shards,
        mesh=paired,
        in_specs=(rows, rows, rows, rows, weight, P()),
        out_specs=(rows, rows, rows, rows, weight),
        check_vma=False,
    )
```
